32 devices in a mesh: parts: 2 (over y), inst: 2 (over core), mesh: 8 (over z, x).
Axes of the slice: x: 2, y: 2, z: 4, core: 2. Of those that a mesh axis runs over, the one named last changes fastest.
Arguments:
- state: float32 [16, 4, 2, 64, 256], P(('parts', 'inst'), None, None, 'mesh'), parts along dimension 0, may hold values from -0.5 to 3, as said below
- donor_rows: int32 [8, 2, 2, 64], P('inst', None, None, 'mesh'), may hold values from 0 to 63, as said below
- donor_weights: float32 [8, 2, 2, 64], P('inst', None, None, 'mesh'), may hold values from 0.2 to 0.8, as said below
Outputs:
- state_next: float32 [16, 4, 2, 64, 256], P(('parts', 'inst'), None, None, 'mesh'), parts along dimension 0
- residual: float32 [16, 4, 2, 64, 256], P(('parts', 'inst'), None, None, 'mesh'), parts along dimension 0
The draws below stay inside these ranges and needn't reach their ends.
There are 2 independent parts, one for each index of `parts`. The reference program is written for one: setup_inputs(seed, part) draws one part's arguments, and reference() takes and returns one part's arrays. A program takes and returns all parts, laid end to end along the dimension named above; an argument that names none is the same for every part. Nothing has to cross between parts.
Inputs may be any that keep to these rules, and one draw needn't show every extreme that they name: `state`: density lies in 0.8 to 1.2, both momenta in -0.5 to 0.5, total energy in 2 to 3. For each instance t and side s there is one offset k with donor_rows[t, s, 0, r] = (r + k) mod 64 and donor_rows[t, s, 1, r] = (r + k + 1) mod 64 for every row r. donor_weights[t, s, 1, r] = 1 - donor_weights[t, s, 0, r].
All inputs are finite; a program needn't handle non-finite values.
Results may differ from the reference program's by a relative error of at most 0.0003.
Values sent between devices are 32-bit elements; how exact they have to be, the bound alone decides.
A program may use at most 128 MiB of HBM per device.

```python
import math
import jax
import jax.numpy as jnp
from jax import lax

NT = 8
NR = 2
NAX = 256
NTH = 64


def draw_state(key, part):
    key = jax.random.fold_in(key, 1)
    low = jnp.array([0.8, -0.5, -0.5, 2.0], jnp.float32).reshape(1, 4, 1, 1, 1)
    high = jnp.array([1.2, 0.5, 0.5, 3.0], jnp.float32).reshape(1, 4, 1, 1, 1)
    fraction = jax.random.uniform(key, (NT, 4, NR, NTH, NAX), jnp.float32)
    return low + (high - low) * fraction


def draw_donor_rows(key, part):
    key = jax.random.fold_in(key, 2)
    offset = jax.random.randint(key, (NT, 2), 0, NTH, dtype=jnp.int32)
    rows = jnp.arange(NTH, dtype=jnp.int32)
    first = jnp.mod(rows[None, None, :] + offset[:, :, None], NTH)
    return jnp.stack([first, jnp.mod(first + 1, NTH)], axis=2).astype(jnp.int32)


def draw_donor_weights(key, part):
    key = jax.random.fold_in(key, 3)
    weight = jax.random.uniform(key, (NT, 2, NTH), jnp.float32, 0.2, 0.8)
    return jnp.stack([weight, 1.0 - weight], axis=2)


def setup_inputs(seed: int = 0, part: int = 0) -> dict:
    key_list = jax.random.split(jax.random.key(seed), 4)
    part_splits = jax.random.split(jax.random.fold_in(key_list[3], part), 4)
    state = draw_state(jax.random.fold_in(jax.random.fold_in(key_list[3], part), 71), part)
    donor_rows = draw_donor_rows(jax.random.fold_in(key_list[3], 71), part)
    donor_weights = draw_donor_weights(jax.random.fold_in(key_list[3], 71), part)
    return dict(state=state, donor_rows=donor_rows, donor_weights=donor_weights)


heat_ratio = 1.4
second_coef = 0.5
fourth_coef = 1.0 / 32.0
time_step = 0.05

def spectral_matrix(mine, theirs, total):
    offset = mine[:, None] - theirs[None, :]
    wrapped = jnp.mod(offset, total)
    parity = 1.0 - 2.0 * jnp.mod(offset, 2).astype(jnp.float32)
    angle = math.pi * offset.astype(jnp.float32) / total
    sine = jnp.where(wrapped == 0, 1.0, jnp.sin(angle))
    return jnp.where(wrapped == 0, 0.0, 0.5 * parity * jnp.cos(angle) / sine).astype(jnp.float32)

def slab(array, start, count, axis):
    return lax.slice_in_dim(array, start, start + count, axis=axis)

def face_sum(padded, axis, normal):
    cells = padded.shape[axis] - 4
    density = padded[:, 0:1]
    axial = padded[:, 1:2]
    circ = padded[:, 2:3]
    energy = padded[:, 3:4]
    pressure = (heat_ratio - 1.0) * (energy - 0.5 * (axial * axial + circ * circ) / density)
    momentum = padded[:, normal:normal + 1]
    speed = momentum / density
    sound = jnp.sqrt(heat_ratio * pressure / density)
    extra_one = pressure if normal == 1 else 0.0
    extra_two = pressure if normal == 2 else 0.0
    flux = jnp.concatenate([momentum, axial * speed + extra_one, circ * speed + extra_two, (energy + pressure) * speed], axis=1)
    radius = jnp.abs(speed) + sound
    upper = slab(pressure, 2, cells + 2, axis)
    center = slab(pressure, 1, cells + 2, axis)
    lower = slab(pressure, 0, cells + 2, axis)
    sensor = jnp.abs(upper - 2.0 * center + lower) / (upper + 2.0 * center + lower)
    eps_two = second_coef * jnp.maximum(slab(sensor, 0, cells + 1, axis), slab(sensor, 1, cells + 1, axis))
    eps_four = jnp.maximum(0.0, fourth_coef - eps_two)
    radius_face = 0.5 * (slab(radius, 1, cells + 1, axis) + slab(radius, 2, cells + 1, axis))
    first = slab(padded, 0, cells + 1, axis)
    second = slab(padded, 1, cells + 1, axis)
    third = slab(padded, 2, cells + 1, axis)
    fourth = slab(padded, 3, cells + 1, axis)
    damping = radius_face * (eps_two * (third - second) - eps_four * (fourth - 3.0 * third + 3.0 * second - first))
    face = 0.5 * (slab(flux, 1, cells + 1, axis) + slab(flux, 2, cells + 1, axis)) - damping
    return slab(face, 1, cells, axis) - slab(face, 0, cells, axis)

def interpolate(source_cols, start, rows, weights):
    span = source_cols.shape[4]
    surfaces = source_cols.shape[3]
    count = rows.shape[0]
    width = rows.shape[3]
    sides = []
    for side in range(2):
        block = source_cols[:, :, 2 * side:2 * side + 2]
        total = jnp.zeros((count, 4, 2, surfaces, width), jnp.float32)
        for point in range(2):
            position = rows[:, side, point, :] - start
            inside = (position >= 0) & (position < span)
            clipped = jnp.clip(position, 0, span - 1).astype(jnp.int32)
            picked = jnp.take_along_axis(block, jnp.broadcast_to(clipped[:, None, None, None, :], (count, 4, 2, surfaces, width)), axis=4)
            weight = weights[:, side, point, :][:, None, None, None, :]
            total = total + jnp.where(inside[:, None, None, None, :], weight * picked, 0.0)
        sides.append(total)
    return jnp.concatenate(sides, axis=2)

def divergence(field, padded_rows, ghost):
    half = field.shape[4] // 2
    rotor_ghost = jnp.moveaxis(ghost[:, :, 0:2], 2, 4)
    stator_ghost = jnp.moveaxis(ghost[:, :, 2:4], 2, 4)
    rotor = jnp.concatenate([field[..., 0:1], field[..., 0:1], field[..., :half], rotor_ghost], axis=4)
    stator = jnp.concatenate([stator_ghost, field[..., half:], field[..., -1:], field[..., -1:]], axis=4)
    axial_part = jnp.concatenate([face_sum(rotor, 4, 1), face_sum(stator, 4, 1)], axis=4)
    return axial_part + face_sum(padded_rows, 3, 2)

def section_residual(field, donor_rows, donor_weights):
    ids = jnp.arange(NT, dtype=jnp.int32)
    matrix = spectral_matrix(ids, ids, NT)
    source = jnp.einsum('tj,jvsrc->tvsrc', matrix, field, precision=lax.Precision.HIGHEST)
    padded_rows = jnp.concatenate([field[:, :, :, -2:], field, field[:, :, :, :2]], axis=3)
    half = field.shape[4] // 2
    piece = jnp.stack([field[..., half], field[..., half + 1], field[..., half - 2], field[..., half - 1]], axis=2)
    ghost = interpolate(piece, 0, donor_rows, donor_weights)

    def one_instance(items):
        return divergence(items[0][None], items[1][None], items[2][None])[0]
    return source + lax.map(one_instance, (field, padded_rows, ghost))

def reference(state, donor_rows, donor_weights):
    first = section_residual(state, donor_rows, donor_weights)
    middle = state - 0.5 * time_step * first
    second = section_residual(middle, donor_rows, donor_weights)
    return (state - time_step * second, second)
```

```python
import functools
import math

import jax
import jax.numpy as jnp
from jax import lax
from jax.experimental import pallas as pl
from jax.experimental.pallas import tpu as pltpu
from jax.sharding import PartitionSpec as P

heat_ratio = 1.4
second_coef = 0.5
fourth_coef = 1.0 / 32.0
time_step = 0.05
LANES = 128
MESH = pl.DeviceIdType.MESH


def spectral(offset, total):
    if offset % total == 0:
        return 0.0
    angle = math.pi * offset / total
    return 0.5 * (1.0 - 2.0 * (offset % 2)) * math.cos(angle) / math.sin(angle)


def primitives(value):
    density, axial, circ, energy = value
    inverse = 1.0 / density
    speed_one = axial * inverse
    speed_two = circ * inverse
    pressure = (heat_ratio - 1.0) * (energy - 0.5 * (axial * speed_one + circ * speed_two))
    sound = jnp.sqrt(heat_ratio * pressure * inverse)
    return pressure, sound, speed_one, speed_two


def flux(value, pressure, speed, normal):
    density, axial, circ, energy = value
    return [
        axial if normal == 1 else circ,
        axial * speed + pressure if normal == 1 else axial * speed,
        circ * speed + pressure if normal == 2 else circ * speed,
        (energy + pressure) * speed,
    ]


def face(cells, pressures, radii, fluxes):
    first, second, third, fourth = pressures
    sensor_one = jnp.abs(third - 2.0 * second + first) / (third + 2.0 * second + first)
    sensor_two = jnp.abs(fourth - 2.0 * third + second) / (fourth + 2.0 * third + second)
    eps_two = second_coef * jnp.maximum(sensor_one, sensor_two)
    eps_four = jnp.maximum(0.0, fourth_coef - eps_two)
    radius = 0.5 * (radii[0] + radii[1])
    two = radius * eps_two
    four = radius * eps_four
    out = []
    for c in range(4):
        step = cells[2][c] - cells[1][c]
        third_diff = cells[3][c] - cells[0][c] - 3.0 * step
        out.append(0.5 * (fluxes[0][c] + fluxes[1][c]) - two * step + four * third_diff)
    return out


def lane_roll(value, shift):
    shift = shift % LANES
    return value if shift == 0 else pltpu.roll(value, shift, 1)


def kernel(
    n, local, surfaces, state_ref, rows_ref, weights_ref, next_ref, res_ref,
    field, other, packed_one, packed_two, prims, acc, ghost, send_sem, recv_sem,
):
    me = lax.axis_index("mesh")
    inst = lax.axis_index("inst")
    partner = 1 - inst
    rows = state_ref.shape[3]
    packed = (packed_one, packed_two)
    lane = lax.broadcasted_iota(jnp.int32, (8, LANES), 1)
    sub = lax.broadcasted_iota(jnp.int32, (8, LANES), 0)
    wide_sub = lax.broadcasted_iota(jnp.int32, (8, 2 * LANES), 0)

    barrier = pltpu.get_barrier_semaphore()

    def greet(k, carry):
        pl.semaphore_signal(
            barrier, inc=1, device_id={"mesh": lax.rem(me + k, n)}, device_id_type=MESH
        )
        return carry

    pl.semaphore_signal(barrier, inc=1, device_id={"inst": partner}, device_id_type=MESH)
    lax.fori_loop(1, n, greet, 0)

    for c in range(4):
        block = jnp.stack([state_ref[t, c, s] for t in range(local) for s in range(surfaces)])
        field[0, c, 2 : 2 + rows] = jnp.swapaxes(block, 0, 1)

    place = lane % 4
    lane_row = lane // 16
    weight = []
    for point in range(2):
        total = jnp.zeros((8, LANES), jnp.float32)
        for t in range(local):
            for side in range(2):
                mine = jnp.zeros((8, LANES), jnp.float32)
                for r in range(rows):
                    mine = jnp.where(lane_row == r, weights_ref[t, side, point, r], mine)
                inside = (sub // surfaces == t) & ((place >= 2) if side == 0 else (place < 2))
                total = jnp.where(inside, mine, total)
        weight.append(total)

    def coefficients(offsets):
        out = jnp.zeros((8, 2 * LANES), jnp.float32)
        for t in range(local):
            out = jnp.where(wide_sub // surfaces == t, spectral(offsets[t], 2 * local), out)
        return out

    own_coef = [
        coefficients([t - (t - k) % local for t in range(local)]) for k in range(local)
    ]
    other_coef = [
        coefficients([local + t - (t - k) % local for t in range(local)]) for k in range(local)
    ]

    def pack(section):
        total = jnp.zeros((8, LANES), jnp.float32)
        for r in range(rows):
            for c in range(4):
                rotor = field[section, c, 2 + r, :, 0:LANES]
                stator = field[section, c, 2 + r, :, LANES : 2 * LANES]
                edge = jnp.where(lane < 2, stator, rotor)
                block = r * 4 + c
                total = jnp.where(lane // 4 == block, lane_roll(edge, block * 4 + 2), total)
        packed[section][me] = total

    def copies(section):
        down = lax.rem(me + n - 1, n)
        up = lax.rem(me + 1, n)
        top = pltpu.make_async_remote_copy(
            field.at[section, :, rows : rows + 2], field.at[section, :, 0:2],
            send_sem.at[section, 0], recv_sem.at[section, 0],
            device_id={"mesh": up}, device_id_type=MESH,
        )
        bottom = pltpu.make_async_remote_copy(
            field.at[section, :, 2:4], field.at[section, :, rows + 2 : rows + 4],
            send_sem.at[section, 1], recv_sem.at[section, 1],
            device_id={"mesh": down}, device_id_type=MESH,
        )
        cross = pltpu.make_async_remote_copy(
            field.at[section, :, 2 : 2 + rows], other.at[section],
            send_sem.at[section, 2], recv_sem.at[section, 2],
            device_id={"inst": partner}, device_id_type=MESH,
        )
        return top, bottom, cross

    def send_columns(section):
        def one(k, carry):
            pltpu.make_async_remote_copy(
                packed[section].at[me], packed[section].at[me],
                send_sem.at[section, 3], recv_sem.at[section, 3],
                device_id={"mesh": lax.rem(me + k, n)}, device_id_type=MESH,
            ).start()
            return carry

        lax.fori_loop(1, n, one, 0)

    def all_columns(section):
        return pltpu.make_async_remote_copy(
            packed[section].at[0 : n - 1], packed[section].at[0 : n - 1],
            send_sem.at[section, 3], recv_sem.at[section, 3],
            device_id={"inst": partner}, device_id_type=MESH,
        )

    def interpolate(section):
        donors = [jnp.zeros((8, LANES), jnp.float32)] * 2
        for t in range(local):
            for side in range(2):
                start = rows_ref[t, side, 0, 0]
                block = start // rows
                offset = start - block * rows
                low = packed[section][block]
                high = packed[section][lax.rem(block + 1, n)]
                inside = (sub // surfaces == t) & ((place >= 2) if side == 0 else (place < 2))
                for point in range(2):
                    shift = (offset + point) * 16
                    picked = jnp.where(lane >= shift, low, high)
                    picked = pltpu.roll(picked, lax.rem(LANES - shift, LANES), 1)
                    donors[point] = jnp.where(inside, picked, donors[point])
        total = weight[0] * donors[0] + weight[1] * donors[1]
        for r in range(rows):
            for c in range(4):
                ghost[r, c] = lane_roll(total, -(r * 4 + c) * 4 - 2)

    def store_primitives(section, row):
        value = [field[section, c, row] for c in range(4)]
        for i, item in enumerate(primitives(value)):
            prims[i, row] = item

    def circ_face(section, row):
        cells = [[field[section, c, row + k] for c in range(4)] for k in (-1, 0, 1, 2)]
        pressures = [prims[0, row + k] for k in (-1, 0, 1, 2)]
        speeds = [prims[3, row + k] for k in (0, 1)]
        radii = [jnp.abs(speeds[k]) + prims[1, row + k] for k in (0, 1)]
        fluxes = [flux(cells[1 + k], pressures[1 + k], speeds[k], 2) for k in (0, 1)]
        return face(cells, pressures, radii, fluxes)

    def axial_term(section, row):
        sides = [
            [field[section, c, row + 2, :, h * LANES : (h + 1) * LANES] for c in range(4)]
            for h in range(2)
        ]
        west, east, ends = [[], []], [[], []], []
        for c in range(4):
            interp = ghost[row, c]
            first = jnp.broadcast_to(sides[0][c][:, 0:1], (8, LANES))
            final = jnp.broadcast_to(sides[1][c][:, LANES - 1 : LANES], (8, LANES))
            low = lane < 64
            west[0].append(jnp.where(low, sides[0][c], first))
            west[1].append(jnp.where(low, sides[1][c], interp))
            east[0].append(jnp.where(low, interp, sides[0][c]))
            east[1].append(jnp.where(low, final, sides[1][c]))
            window = west[0][c]
            for source, shift in ((east[0][c], 32), (west[1][c], 64), (east[1][c], 96)):
                inside = (lane >= shift - 16) & (lane < shift + 16)
                window = jnp.where(inside, lane_roll(source, shift), window)
            ends.append(window)
        end_pressure, end_sound, end_speed, _ = primitives(ends)
        end_radius = jnp.abs(end_speed) + end_sound
        end_flux = flux(ends, end_pressure, end_speed, 1)

        def moved(value, shift):
            return [lane_roll(v, shift) for v in value]

        end_face = face(
            [moved(ends, 1), ends, moved(ends, -1), moved(ends, -2)],
            [lane_roll(end_pressure, s) for s in (1, 0, -1, -2)],
            [end_radius, lane_roll(end_radius, -1)],
            [end_flux, moved(end_flux, -1)],
        )
        out = []
        for h in range(2):
            cut = slice(h * LANES, (h + 1) * LANES)
            value = sides[h]
            pressure = prims[0, row + 2, :, cut]
            sound = prims[1, row + 2, :, cut]
            speed = prims[2, row + 2, :, cut]
            radius = jnp.abs(speed) + sound
            flow = flux(value, pressure, speed, 1)
            shift_west, shift_east = 64 * h, 32 + 64 * h
            before_p = lane_roll(end_pressure, -shift_west)
            after_p = lane_roll(end_pressure, -shift_east)

            def previous(own, edge):
                return lane_roll(jnp.where(lane == LANES - 1, edge, own), 1)

            def second_next(own, edge):
                return lane_roll(jnp.where(lane == 0, edge, own), -2)

            main = face(
                [
                    [previous(value[c], west[h][c]) for c in range(4)],
                    value,
                    moved(value, -1),
                    [second_next(value[c], east[h][c]) for c in range(4)],
                ],
                [
                    previous(pressure, before_p),
                    pressure,
                    lane_roll(pressure, -1),
                    second_next(pressure, after_p),
                ],
                [radius, lane_roll(radius, -1)],
                [flow, moved(flow, -1)],
            )
            part = []
            for c in range(4):
                right = jnp.where(lane == LANES - 1, lane_roll(end_face[c], -shift_east), main[c])
                left = previous(main[c], lane_roll(end_face[c], -shift_west))
                part.append(right - left)
            out.append(part)
        return [jnp.concatenate([out[0][c], out[1][c]], axis=1) for c in range(4)]

    def own_part(section, row):
        store_primitives(section, row + 2)
        for c in range(4):
            value = field[section, c, row + 2]
            total = own_coef[1] * pltpu.roll(value, surfaces, 0)
            for k in range(2, local):
                total += own_coef[k] * pltpu.roll(value, surfaces * k, 0)
            acc[c, row] = total

    def run(section):
        top, bottom, cross = copies(section)
        top.start()
        bottom.start()
        pack(section)
        send_columns(section)
        cross.start()

        def prepare(row, carry):
            own_part(section, row)
            return carry

        lax.fori_loop(0, rows, prepare, 0)
        cross.wait_recv()

        def others(row, carry):
            for c in range(4):
                value = other[section, c, row]
                total = acc[c, row] + other_coef[0] * value
                for k in range(1, local):
                    total += other_coef[k] * pltpu.roll(value, surfaces * k, 0)
                acc[c, row] = total
            return carry

        lax.fori_loop(0, rows, others, 0)
        all_columns(section).wait_recv()
        interpolate(section)

        def axial(row, carry):
            term = axial_term(section, row)
            for c in range(4):
                acc[c, row] += term[c]
            return carry

        lax.fori_loop(0, rows, axial, 0)
        top.wait_recv()
        bottom.wait_recv()
        for row in (0, 1, rows + 2, rows + 3):
            store_primitives(section, row)

        def circ(row, left):
            right = circ_face(section, row + 2)
            for c in range(4):
                total = acc[c, row] + (right[c] - left[c])
                if section == 0:
                    field[1, c, row + 2] = field[0, c, row + 2] - 0.5 * time_step * total
                else:
                    acc[c, row] = total
            return right

        lax.fori_loop(0, rows, circ, circ_face(section, 1))

    pl.semaphore_wait(barrier, n)
    run(0)
    run(1)
    for c in range(4):
        block = jnp.swapaxes(acc[c], 0, 1)
        for t in range(local):
            for s in range(surfaces):
                value = block[t * surfaces + s]
                res_ref[t, c, s] = value
                next_ref[t, c, s] = state_ref[t, c, s] - time_step * value
    for section in range(2):
        for copy in copies(section):
            copy.wait_send()
        all_columns(section).wait_send()


def per_device(n, state, donor_rows, donor_weights):
    local, _, surfaces, rows, columns = state.shape
    shape = jax.ShapeDtypeStruct(state.shape, jnp.float32)
    vmem = pl.BlockSpec(memory_space=pltpu.VMEM)
    smem = pl.BlockSpec(memory_space=pltpu.SMEM)
    return tuple(
        pl.pallas_call(
            functools.partial(kernel, n, local, surfaces),
            out_shape=[shape, shape],
            in_specs=[vmem, smem, smem],
            out_specs=[vmem, vmem],
            scratch_shapes=[
                pltpu.VMEM((2, 4, rows + 4, 8, columns), jnp.float32),
                pltpu.VMEM((2, 4, rows, 8, columns), jnp.float32),
                pltpu.VMEM((n, 8, LANES), jnp.float32),
                pltpu.VMEM((n, 8, LANES), jnp.float32),
                pltpu.VMEM((4, rows + 4, 8, columns), jnp.float32),
                pltpu.VMEM((4, rows, 8, columns), jnp.float32),
                pltpu.VMEM((rows, 4, 8, LANES), jnp.float32),
                pltpu.SemaphoreType.DMA((2, 4)),
                pltpu.SemaphoreType.DMA((2, 4)),
            ],
            compiler_params=pltpu.CompilerParams(
                collective_id=0, has_side_effects=True, vmem_limit_bytes=24 * 2**20
            ),
        )(state, donor_rows, donor_weights)
    )


def solution(mesh):
    return jax.shard_map(
        functools.partial(per_device, mesh.shape["mesh"]),
        mesh=mesh,
        in_specs=(
            P(("parts", "inst"), None, None, "mesh", None),
            P("inst", None, None, "mesh"),
            P("inst", None, None, "mesh"),
        ),
        out_specs=(
            P(("parts", "inst"), None, None, "mesh", None),
            P(("parts", "inst"), None, None, "mesh", None),
        ),
        check_vma=False,
    )
```

```python
import functools
import math

import jax
import jax.numpy as jnp
from jax import lax
from jax.experimental import pallas as pl
from jax.experimental.pallas import tpu as pltpu
from jax.sharding import PartitionSpec as P

heat_ratio = 1.4
second_coef = 0.5
fourth_coef = 1.0 / 32.0
time_step = 0.05
LANES = 128
MESH = pl.DeviceIdType.MESH


def spectral(offset, total):
    if offset % total == 0:
        return 0.0
    angle = math.pi * offset / total
    return 0.5 * (1.0 - 2.0 * (offset % 2)) * math.cos(angle) / math.sin(angle)


def primitives(value):
    density, axial, circ, energy = value
    inverse = 1.0 / density
    speed_one = axial * inverse
    speed_two = circ * inverse
    pressure = (heat_ratio - 1.0) * (energy - 0.5 * (axial * speed_one + circ * speed_two))
    sound = jnp.sqrt(heat_ratio * pressure * inverse)
    return pressure, sound, speed_one, speed_two


def flux(value, pressure, speed, normal):
    density, axial, circ, energy = value
    return [
        axial if normal == 1 else circ,
        axial * speed + pressure if normal == 1 else axial * speed,
        circ * speed + pressure if normal == 2 else circ * speed,
        (energy + pressure) * speed,
    ]


def sensor(before, center, after):
    twice = 2.0 * center
    return jnp.abs(after - twice + before) / (after + twice + before)


def face(cells, sensors, radii, fluxes):
    eps_two = second_coef * jnp.maximum(sensors[0], sensors[1])
    eps_four = jnp.maximum(0.0, fourth_coef - eps_two)
    radius = 0.5 * (radii[0] + radii[1])
    two = radius * eps_two
    four = radius * eps_four
    out = []
    for c in range(4):
        step = cells[2][c] - cells[1][c]
        third_diff = cells[3][c] - cells[0][c] - 3.0 * step
        out.append(0.5 * (fluxes[0][c] + fluxes[1][c]) - two * step + four * third_diff)
    return out


def lane_roll(value, shift):
    shift = shift % LANES
    return value if shift == 0 else pltpu.roll(value, shift, 1)


def kernel(
    n, local, surfaces, state_in, rows_in, weights_in, half_ref,
    state_ref, rows_ref, weights_ref, field, other, packed_one, packed_two, prims, acc, edges,
    local_sem, send_sem, recv_sem,
):
    me = lax.axis_index("mesh")
    inst = lax.axis_index("inst")
    partner = 1 - inst
    rows = state_ref.shape[3]
    packed = (packed_one, packed_two)
    lane = lax.broadcasted_iota(jnp.int32, (8, LANES), 1)
    sub = lax.broadcasted_iota(jnp.int32, (8, LANES), 0)
    wide_sub = lax.broadcasted_iota(jnp.int32, (8, 2 * LANES), 0)

    loads = [
        pltpu.make_async_copy(source, target, local_sem.at[i])
        for i, (source, target) in enumerate(
            ((state_in, state_ref), (rows_in, rows_ref), (weights_in, weights_ref))
        )
    ]
    for load in loads:
        load.start()
    barrier = pltpu.get_barrier_semaphore()

    def greet(k, carry):
        pl.semaphore_signal(
            barrier, inc=1, device_id={"mesh": lax.rem(me + k, n)}, device_id_type=MESH
        )
        return carry

    pl.semaphore_signal(barrier, inc=1, device_id={"inst": partner}, device_id_type=MESH)
    lax.fori_loop(1, n, greet, 0)

    loads[0].wait()
    for c in range(4):
        block = jnp.stack([state_ref[t, c, s] for t in range(local) for s in range(surfaces)])
        field[0, c, 2 : 2 + rows] = jnp.swapaxes(block, 0, 1)

    loads[1].wait()
    loads[2].wait()
    place = lane % 4
    lane_row = lane // 16
    weight = []
    for point in range(2):
        total = jnp.zeros((8, LANES), jnp.float32)
        for t in range(local):
            for side in range(2):
                mine = jnp.zeros((8, LANES), jnp.float32)
                for r in range(rows):
                    mine = jnp.where(lane_row == r, weights_ref[t, side, point, r], mine)
                inside = (sub // surfaces == t) & ((place >= 2) if side == 0 else (place < 2))
                total = jnp.where(inside, mine, total)
        weight.append(total)

    def coefficients(offsets):
        out = jnp.zeros((8, 2 * LANES), jnp.float32)
        for t in range(local):
            out = jnp.where(wide_sub // surfaces == t, spectral(offsets[t], 2 * local), out)
        return out

    own_coef = [None] + [
        coefficients([t - (t - k) % local for t in range(local)]) for k in range(1, local)
    ]
    other_coef = [
        coefficients([local + t - (t - k) % local for t in range(local)]) for k in range(local)
    ]

    spot = lane % 16

    def pack(section):
        out = []
        for c in range(4):
            total = jnp.zeros((8, LANES), jnp.float32)
            for r in range(rows):
                rotor = field[section, c, 2 + r, :, 0:LANES]
                stator = field[section, c, 2 + r, :, LANES : 2 * LANES]
                edge = jnp.where(lane < 64, stator, rotor)
                total = jnp.where(lane_row == r, lane_roll(edge, r * 16 + 3), total)
            edges[section, c] = total
            out.append(total)
        total = lane_roll(out[0], -1)
        for c in range(1, 4):
            total = jnp.where(spot // 4 == c, lane_roll(out[c], c * 4 - 1), total)
        packed[section][me] = total

    def copies(section):
        down = lax.rem(me + n - 1, n)
        up = lax.rem(me + 1, n)
        top = pltpu.make_async_remote_copy(
            field.at[section, :, rows : rows + 2], field.at[section, :, 0:2],
            send_sem.at[section, 0], recv_sem.at[section, 0],
            device_id={"mesh": up}, device_id_type=MESH,
        )
        bottom = pltpu.make_async_remote_copy(
            field.at[section, :, 2:4], field.at[section, :, rows + 2 : rows + 4],
            send_sem.at[section, 1], recv_sem.at[section, 1],
            device_id={"mesh": down}, device_id_type=MESH,
        )
        cross = pltpu.make_async_remote_copy(
            field.at[section, :, 2 : 2 + rows], other.at[section],
            send_sem.at[section, 2], recv_sem.at[section, 2],
            device_id={"inst": partner}, device_id_type=MESH,
        )
        return top, bottom, cross

    def send_columns(section):
        def one(k, carry):
            pltpu.make_async_remote_copy(
                packed[section].at[me], packed[section].at[me],
                send_sem.at[section, 3], recv_sem.at[section, 3],
                device_id={"mesh": lax.rem(me + k, n)}, device_id_type=MESH,
            ).start()
            return carry

        lax.fori_loop(1, n, one, 0)

    def all_columns(section):
        return pltpu.make_async_remote_copy(
            packed[section].at[0 : n - 1], packed[section].at[0 : n - 1],
            send_sem.at[section, 3], recv_sem.at[section, 3],
            device_id={"inst": partner}, device_id_type=MESH,
        )

    def interpolate(section):
        donors = [jnp.zeros((8, LANES), jnp.float32)] * 2
        for t in range(local):
            for side in range(2):
                start = rows_ref[t, side, 0, 0]
                block = start // rows
                offset = start - block * rows
                low = packed[section][block]
                high = packed[section][lax.rem(block + 1, n)]
                inside = (sub // surfaces == t) & ((place >= 2) if side == 0 else (place < 2))
                for point in range(2):
                    shift = (offset + point) * 16
                    picked = jnp.where(lane >= shift, low, high)
                    picked = pltpu.roll(picked, lax.rem(LANES - shift, LANES), 1)
                    donors[point] = jnp.where(inside, picked, donors[point])
        total = weight[0] * donors[0] + weight[1] * donors[1]
        window = []
        for c in range(4):
            near = edges[section, c]
            value = jnp.where(spot < 3, near, lane_roll(near, 7))
            value = jnp.where((spot == 3) | (spot == 4), lane_roll(total, 1 - 4 * c), value)
            value = jnp.where((spot == 8) | (spot == 9), lane_roll(total, 8 - 4 * c), value)
            window.append(jnp.where((spot < 5) | ((spot >= 8) & (spot < 13)), value, near_one[c]))
        pressure, sound, speed, _ = primitives(window)
        radius = jnp.abs(speed) + sound
        flow = flux(window, pressure, speed, 1)
        sense = sensor(lane_roll(pressure, 1), pressure, lane_roll(pressure, -1))
        edge_face = face(
            [moved(window, 1), window, moved(window, -1), moved(window, -2)],
            [sense, lane_roll(sense, -1)],
            [radius, lane_roll(radius, -1)],
            [flow, moved(flow, -1)],
        )
        valid = (spot == 1) | (spot == 2) | (spot == 9) | (spot == 10)
        fix = []
        for c in range(4):
            value = jnp.where(valid, edge_face[c], 0.0)
            value = value - lane_roll(value, 1)
            fix.append(jnp.where(spot < 3, value, lane_roll(value, -7)))
        for c in range(4):
            for r in range(rows):
                moved_back = lane_roll(fix[c], -(r * 16 + 3))
                acc[c, r, :, 0:LANES] += jnp.where(lane >= LANES - 2, moved_back, 0.0)
                acc[c, r, :, LANES : 2 * LANES] += jnp.where(lane < 2, moved_back, 0.0)

    near_one = [1.0, 0.0, 0.0, 2.0]

    def moved(value, shift):
        return [lane_roll(v, shift) for v in value]

    def store_primitives(section, row):
        value = [field[section, c, row] for c in range(4)]
        for i, item in enumerate(primitives(value)):
            prims[i, row] = item

    def row_sensor(row):
        return sensor(prims[0, row - 1], prims[0, row], prims[0, row + 1])

    def circ_face(section, row, before):
        after = row_sensor(row + 1)
        cells = [[field[section, c, row + k] for c in range(4)] for k in (-1, 0, 1, 2)]
        speeds = [prims[3, row + k] for k in (0, 1)]
        radii = [jnp.abs(speeds[k]) + prims[1, row + k] for k in (0, 1)]
        fluxes = [flux(cells[1 + k], prims[0, row + k], speeds[k], 2) for k in (0, 1)]
        return face(cells, [before, after], radii, fluxes), after

    def axial_half(section, row, h):
        cut = slice(h * LANES, (h + 1) * LANES)
        value = [field[section, c, row + 2, :, cut] for c in range(4)]
        pressure = prims[0, row + 2, :, cut]
        speed = prims[2, row + 2, :, cut]
        radius = jnp.abs(speed) + prims[1, row + 2, :, cut]
        flow = flux(value, pressure, speed, 1)
        first, last = lane == 0, lane == LANES - 1

        def before(own):
            return jnp.where(first, own, lane_roll(own, 1)) if h == 0 else lane_roll(own, 1)

        def after(own):
            return jnp.where(last, own, lane_roll(own, -1)) if h == 1 else lane_roll(own, -1)

        following = [after(v) for v in value]
        second = moved(value, -2)
        if h == 1:
            second = [jnp.where(lane >= LANES - 2, a, b) for a, b in zip(following, second)]
        sense = sensor(before(pressure), pressure, after(pressure))
        sense_after = lane_roll(sense, -1)
        if h == 1:
            sense_after = jnp.where(last, 0.0, sense_after)
        right = face(
            [[before(v) for v in value], value, following, second],
            [sense, sense_after],
            [radius, after(radius)],
            [flow, [after(f) for f in flow]],
        )
        keep = lane < LANES - 2 if h == 0 else lane > 0
        right = [jnp.where(keep, f, 0.0) for f in right]
        if h == 0:
            four = radius * jnp.maximum(0.0, fourth_coef - second_coef * sense)
            start = [flow[c] + four * (following[c] - value[c]) for c in range(4)]
        else:
            start = [0.0] * 4
        return [right[c] - jnp.where(first, start[c], lane_roll(right[c], 1)) for c in range(4)]

    def source(values, coefs, total):
        for k, coef in enumerate(coefs):
            if coef is not None:
                value = values if k == 0 else pltpu.roll(values, surfaces * k, 0)
                total = coef * value if total is None else total + coef * value
        return total

    def alone(section):
        def one(row, carry):
            store_primitives(section, row + 2)
            halves = [axial_half(section, row, h) for h in range(2)]
            for c in range(4):
                term = jnp.concatenate([halves[0][c], halves[1][c]], axis=1)
                acc[c, row] = source(field[section, c, row + 2], own_coef, term)
            return carry

        lax.fori_loop(0, rows, one, 0, unroll=2)

    def send(section):
        top, bottom, cross = copies(section)
        top.start()
        bottom.start()
        send_columns(section)
        cross.start()

    def together(section):
        top, bottom, cross = copies(section)
        cross.wait_recv()

        def others(row, carry):
            for c in range(4):
                acc[c, row] = source(other[section, c, row], other_coef, acc[c, row])
            return carry

        lax.fori_loop(0, rows, others, 0, unroll=2)
        all_columns(section).wait_recv()
        interpolate(section)
        top.wait_recv()
        bottom.wait_recv()
        for row in (0, 1, rows + 2, rows + 3):
            store_primitives(section, row)

        def circ(row, carry):
            left, sense = carry
            right, sense = circ_face(section, row + 2, sense)
            for c in range(4):
                total = acc[c, row] + (right[c] - left[c])
                if section == 0:
                    field[1, c, row + 2] = field[0, c, row + 2] - 0.5 * time_step * total
                else:
                    acc[c, row] = 0.5 * total
            return right, sense

        lax.fori_loop(0, rows, circ, circ_face(section, 1, row_sensor(1)))

    pack(0)
    alone(0)
    pl.semaphore_wait(barrier, n)
    send(0)
    together(0)
    pack(1)
    send(1)
    alone(1)
    together(1)
    for c in range(4):
        block = jnp.swapaxes(acc[c], 0, 1)
        for t in range(local):
            for s in range(surfaces):
                half_ref[t, c, s] = block[t * surfaces + s]
    for section in range(2):
        for copy in copies(section):
            copy.wait_send()
        all_columns(section).wait_send()


def per_device(n, state, donor_rows, donor_weights):
    local, _, surfaces, rows, columns = state.shape
    half = pl.pallas_call(
        functools.partial(kernel, n, local, surfaces),
        out_shape=jax.ShapeDtypeStruct(state.shape, jnp.float32),
        in_specs=[pl.BlockSpec(memory_space=pltpu.HBM)] * 3,
        out_specs=pl.BlockSpec(memory_space=pltpu.VMEM),
        scratch_shapes=[
            pltpu.VMEM(state.shape, jnp.float32),
            pltpu.SMEM(donor_rows.shape, jnp.int32),
            pltpu.SMEM(donor_weights.shape, jnp.float32),
            pltpu.VMEM((2, 4, rows + 4, 8, columns), jnp.float32),
            pltpu.VMEM((2, 4, rows, 8, columns), jnp.float32),
            pltpu.VMEM((n, 8, LANES), jnp.float32),
            pltpu.VMEM((n, 8, LANES), jnp.float32),
            pltpu.VMEM((4, rows + 4, 8, columns), jnp.float32),
            pltpu.VMEM((4, rows, 8, columns), jnp.float32),
            pltpu.VMEM((2, 4, 8, LANES), jnp.float32),
            pltpu.SemaphoreType.DMA((3,)),
            pltpu.SemaphoreType.DMA((2, 4)),
            pltpu.SemaphoreType.DMA((2, 4)),
        ],
        compiler_params=pltpu.CompilerParams(
            collective_id=0, has_side_effects=True, vmem_limit_bytes=24 * 2**20
        ),
    )(state, donor_rows, donor_weights)
    return state - (2.0 * time_step) * half, half + half


def solution(mesh):
    return jax.shard_map(
        functools.partial(per_device, mesh.shape["mesh"]),
        mesh=mesh,
        in_specs=(
            P(("parts", "inst"), None, None, "mesh", None),
            P("inst", None, None, "mesh"),
            P("inst", None, None, "mesh"),
        ),
        out_specs=(
            P(("parts", "inst"), None, None, "mesh", None),
            P(("parts", "inst"), None, None, "mesh", None),
        ),
        check_vma=False,
    )
```

```python
import functools
import math

import jax
import jax.numpy as jnp
from jax import lax
from jax.experimental import pallas as pl
from jax.experimental.pallas import tpu as pltpu
from jax.sharding import PartitionSpec as P

heat_ratio = 1.4
second_coef = 0.5
fourth_coef = 1.0 / 32.0
time_step = 0.05
LANES = 128
MESH = pl.DeviceIdType.MESH


def spectral(offset, total):
    if offset % total == 0:
        return 0.0
    angle = math.pi * offset / total
    return 0.5 * (1.0 - 2.0 * (offset % 2)) * math.cos(angle) / math.sin(angle)


def primitives(value):
    density, axial, circ, energy = value
    inverse = 1.0 / density
    speed_one = axial * inverse
    speed_two = circ * inverse
    pressure = (heat_ratio - 1.0) * (energy - 0.5 * (axial * speed_one + circ * speed_two))
    sound = jnp.sqrt(heat_ratio * pressure * inverse)
    return pressure, sound, speed_one, speed_two


def flux(value, pressure, speed, normal):
    density, axial, circ, energy = value
    return [
        axial if normal == 1 else circ,
        axial * speed + pressure if normal == 1 else axial * speed,
        circ * speed + pressure if normal == 2 else circ * speed,
        (energy + pressure) * speed,
    ]


def sensor(before, center, after):
    twice = 2.0 * center
    return jnp.abs(after - twice + before) / (after + twice + before)


def face(cells, sensors, radii, fluxes):
    eps_two = second_coef * jnp.maximum(sensors[0], sensors[1])
    eps_four = jnp.maximum(0.0, fourth_coef - eps_two)
    radius = 0.5 * (radii[0] + radii[1])
    two = radius * eps_two
    four = radius * eps_four
    out = []
    for c in range(4):
        step = cells[2][c] - cells[1][c]
        third_diff = cells[3][c] - cells[0][c] - 3.0 * step
        out.append(0.5 * (fluxes[0][c] + fluxes[1][c]) - two * step + four * third_diff)
    return out


def lane_roll(value, shift):
    shift = shift % LANES
    return value if shift == 0 else pltpu.roll(value, shift, 1)


def kernel(
    n, local, surfaces, state_in, rows_in, weights_in, half_ref,
    state_ref, rows_ref, weights_ref, field, other, packed_one, packed_two, prims, acc, edges,
    local_sem, send_sem, recv_sem,
):
    me = lax.axis_index("mesh")
    inst = lax.axis_index("inst")
    partner = 1 - inst
    rows = state_ref.shape[3]
    packed = (packed_one, packed_two)
    lane = lax.broadcasted_iota(jnp.int32, (8, LANES), 1)
    sub = lax.broadcasted_iota(jnp.int32, (8, LANES), 0)
    wide_sub = lax.broadcasted_iota(jnp.int32, (8, 2 * LANES), 0)

    loads = [
        pltpu.make_async_copy(source, target, local_sem.at[i])
        for i, (source, target) in enumerate(
            ((state_in, state_ref), (rows_in, rows_ref), (weights_in, weights_ref))
        )
    ]
    for load in loads:
        load.start()
    barrier = pltpu.get_barrier_semaphore()

    def greet(k, carry):
        pl.semaphore_signal(
            barrier, inc=1, device_id={"mesh": lax.rem(me + k, n)}, device_id_type=MESH
        )
        return carry

    pl.semaphore_signal(barrier, inc=1, device_id={"inst": partner}, device_id_type=MESH)
    lax.fori_loop(1, n, greet, 0)

    loads[0].wait()
    for c in range(4):
        block = jnp.stack([state_ref[t, c, s] for t in range(local) for s in range(surfaces)])
        field[0, c, 2 : 2 + rows] = jnp.swapaxes(block, 0, 1)

    loads[1].wait()
    loads[2].wait()
    place = lane % 4
    lane_row = lane // 16
    weight = []
    for point in range(2):
        total = jnp.zeros((8, LANES), jnp.float32)
        for t in range(local):
            for side in range(2):
                mine = jnp.zeros((8, LANES), jnp.float32)
                for r in range(rows):
                    mine = jnp.where(lane_row == r, weights_ref[t, side, point, r], mine)
                inside = (sub // surfaces == t) & ((place >= 2) if side == 0 else (place < 2))
                total = jnp.where(inside, mine, total)
        weight.append(total)

    def coefficients(offsets):
        out = jnp.zeros((8, 2 * LANES), jnp.float32)
        for t in range(local):
            out = jnp.where(wide_sub // surfaces == t, spectral(offsets[t], 2 * local), out)
        return out

    own_coef = [None] + [
        coefficients([t - (t - k) % local for t in range(local)]) for k in range(1, local)
    ]
    other_coef = [
        coefficients([local + t - (t - k) % local for t in range(local)]) for k in range(local)
    ]

    spot = lane % 16

    def pack(section):
        out = []
        for c in range(4):
            total = jnp.zeros((8, LANES), jnp.float32)
            for r in range(rows):
                rotor = field[section, c, 2 + r, :, 0:LANES]
                stator = field[section, c, 2 + r, :, LANES : 2 * LANES]
                edge = jnp.where(lane < 64, stator, rotor)
                total = jnp.where(lane_row == r, lane_roll(edge, r * 16 + 3), total)
            edges[section, c] = total
            out.append(total)
        total = lane_roll(out[0], -1)
        for c in range(1, 4):
            total = jnp.where(spot // 4 == c, lane_roll(out[c], c * 4 - 1), total)
        packed[section][me] = total

    def copies(section):
        down = lax.rem(me + n - 1, n)
        up = lax.rem(me + 1, n)
        top = pltpu.make_async_remote_copy(
            field.at[section, :, rows : rows + 2], field.at[section, :, 0:2],
            send_sem.at[section, 0], recv_sem.at[section, 0],
            device_id={"mesh": up}, device_id_type=MESH,
        )
        bottom = pltpu.make_async_remote_copy(
            field.at[section, :, 2:4], field.at[section, :, rows + 2 : rows + 4],
            send_sem.at[section, 1], recv_sem.at[section, 1],
            device_id={"mesh": down}, device_id_type=MESH,
        )
        cross = pltpu.make_async_remote_copy(
            field.at[section, :, 2 : 2 + rows], other.at[section],
            send_sem.at[section, 2], recv_sem.at[section, 2],
            device_id={"inst": partner}, device_id_type=MESH,
        )
        return top, bottom, cross

    def send_columns(section):
        def one(k, carry):
            pltpu.make_async_remote_copy(
                packed[section].at[me], packed[section].at[me],
                send_sem.at[section, 3], recv_sem.at[section, 3],
                device_id={"mesh": lax.rem(me + k, n)}, device_id_type=MESH,
            ).start()
            return carry

        lax.fori_loop(1, n, one, 0)

    def all_columns(section):
        return pltpu.make_async_remote_copy(
            packed[section].at[0 : n - 1], packed[section].at[0 : n - 1],
            send_sem.at[section, 3], recv_sem.at[section, 3],
            device_id={"inst": partner}, device_id_type=MESH,
        )

    def interpolate(section):
        donors = [jnp.zeros((8, LANES), jnp.float32)] * 2
        for t in range(local):
            for side in range(2):
                start = rows_ref[t, side, 0, 0]
                block = start // rows
                offset = start - block * rows
                low = packed[section][block]
                high = packed[section][lax.rem(block + 1, n)]
                inside = (sub // surfaces == t) & ((place >= 2) if side == 0 else (place < 2))
                for point in range(2):
                    shift = (offset + point) * 16
                    picked = jnp.where(lane >= shift, low, high)
                    picked = pltpu.roll(picked, lax.rem(LANES - shift, LANES), 1)
                    donors[point] = jnp.where(inside, picked, donors[point])
        total = weight[0] * donors[0] + weight[1] * donors[1]
        window = []
        for c in range(4):
            near = edges[section, c]
            value = jnp.where(spot < 3, near, lane_roll(near, 7))
            value = jnp.where((spot == 3) | (spot == 4), lane_roll(total, 1 - 4 * c), value)
            value = jnp.where((spot == 8) | (spot == 9), lane_roll(total, 8 - 4 * c), value)
            window.append(jnp.where((spot < 5) | ((spot >= 8) & (spot < 13)), value, near_one[c]))
        pressure, sound, speed, _ = primitives(window)
        radius = jnp.abs(speed) + sound
        flow = flux(window, pressure, speed, 1)
        sense = sensor(lane_roll(pressure, 1), pressure, lane_roll(pressure, -1))
        edge_face = face(
            [moved(window, 1), window, moved(window, -1), moved(window, -2)],
            [sense, lane_roll(sense, -1)],
            [radius, lane_roll(radius, -1)],
            [flow, moved(flow, -1)],
        )
        valid = (spot == 1) | (spot == 2) | (spot == 9) | (spot == 10)
        fix = []
        for c in range(4):
            value = jnp.where(valid, edge_face[c], 0.0)
            value = value - lane_roll(value, 1)
            fix.append(jnp.where(spot < 3, value, lane_roll(value, -7)))
        for c in range(4):
            for r in range(rows):
                moved_back = lane_roll(fix[c], -(r * 16 + 3))
                acc[c, r, :, 0:LANES] += jnp.where(lane >= LANES - 2, moved_back, 0.0)
                acc[c, r, :, LANES : 2 * LANES] += jnp.where(lane < 2, moved_back, 0.0)

    near_one = [1.0, 0.0, 0.0, 2.0]

    def moved(value, shift):
        return [lane_roll(v, shift) for v in value]

    def store_primitives(section, row):
        value = [field[section, c, row] for c in range(4)]
        for i, item in enumerate(primitives(value)):
            prims[i, row] = item

    def row_sensor(row):
        return sensor(prims[0, row - 1], prims[0, row], prims[0, row + 1])

    def circ_face(section, row, before):
        after = row_sensor(row + 1)
        cells = [[field[section, c, row + k] for c in range(4)] for k in (-1, 0, 1, 2)]
        speeds = [prims[3, row + k] for k in (0, 1)]
        radii = [jnp.abs(speeds[k]) + prims[1, row + k] for k in (0, 1)]
        fluxes = [flux(cells[1 + k], prims[0, row + k], speeds[k], 2) for k in (0, 1)]
        return face(cells, [before, after], radii, fluxes), after

    def axial_half(section, row, h):
        cut = slice(h * LANES, (h + 1) * LANES)
        value = [field[section, c, row + 2, :, cut] for c in range(4)]
        pressure = prims[0, row + 2, :, cut]
        speed = prims[2, row + 2, :, cut]
        radius = jnp.abs(speed) + prims[1, row + 2, :, cut]
        flow = flux(value, pressure, speed, 1)
        first, last = lane == 0, lane == LANES - 1

        def before(own):
            return jnp.where(first, own, lane_roll(own, 1)) if h == 0 else lane_roll(own, 1)

        def after(own):
            return jnp.where(last, own, lane_roll(own, -1)) if h == 1 else lane_roll(own, -1)

        following = [after(v) for v in value]
        second = moved(value, -2)
        if h == 1:
            second = [jnp.where(lane >= LANES - 2, a, b) for a, b in zip(following, second)]
        sense = sensor(before(pressure), pressure, after(pressure))
        sense_after = lane_roll(sense, -1)
        if h == 1:
            sense_after = jnp.where(last, 0.0, sense_after)
        right = face(
            [[before(v) for v in value], value, following, second],
            [sense, sense_after],
            [radius, after(radius)],
            [flow, [after(f) for f in flow]],
        )
        keep = lane < LANES - 2 if h == 0 else lane > 0
        right = [jnp.where(keep, f, 0.0) for f in right]
        if h == 0:
            four = radius * jnp.maximum(0.0, fourth_coef - second_coef * sense)
            start = [flow[c] + four * (following[c] - value[c]) for c in range(4)]
        else:
            start = [0.0] * 4
        return [right[c] - jnp.where(first, start[c], lane_roll(right[c], 1)) for c in range(4)]

    def source(values, coefs, total):
        for k, coef in enumerate(coefs):
            if coef is not None:
                value = values if k == 0 else pltpu.roll(values, surfaces * k, 0)
                total = coef * value if total is None else total + coef * value
        return total

    def alone(section):
        def one(row, carry):
            store_primitives(section, row + 2)
            halves = [axial_half(section, row, h) for h in range(2)]
            for c in range(4):
                term = jnp.concatenate([halves[0][c], halves[1][c]], axis=1)
                acc[c, row] = source(field[section, c, row + 2], own_coef, term)
            return carry

        lax.fori_loop(0, rows, one, 0, unroll=2)

    def send(section):
        top, bottom, cross = copies(section)
        top.start()
        bottom.start()
        send_columns(section)
        cross.start()

    def together(section):
        top, bottom, cross = copies(section)
        cross.wait_recv()

        def others(row, carry):
            for c in range(4):
                acc[c, row] = source(other[section, c, row], other_coef, acc[c, row])
            return carry

        lax.fori_loop(0, rows, others, 0, unroll=2)
        all_columns(section).wait_recv()
        interpolate(section)
        top.wait_recv()
        bottom.wait_recv()
        for row in (0, 1, rows + 2, rows + 3):
            store_primitives(section, row)

        def circ(row, carry):
            left, sense = carry
            right, sense = circ_face(section, row + 2, sense)
            for c in range(4):
                total = acc[c, row] + (right[c] - left[c])
                if section == 0:
                    field[1, c, row + 2] = field[0, c, row + 2] - 0.5 * time_step * total
                else:
                    acc[c, row] = 0.5 * total
            return right, sense

        lax.fori_loop(0, rows, circ, circ_face(section, 1, row_sensor(1)))

    pack(0)
    alone(0)
    pl.semaphore_wait(barrier, n)
    send(0)
    together(0)
    pack(1)
    send(1)
    alone(1)
    together(1)
    for c in range(4):
        block = jnp.swapaxes(acc[c], 0, 1)
        for t in range(local):
            for s in range(surfaces):
                half_ref[t, c, s] = block[t * surfaces + s]
    for section in range(2):
        for copy in copies(section):
            copy.wait_send()
        all_columns(section).wait_send()


def per_device(n, state, donor_rows, donor_weights):
    local, _, surfaces, rows, columns = state.shape
    inputs = [
        pltpu.with_memory_space_constraint(x, pltpu.HBM)
        for x in (state, donor_rows, donor_weights)
    ]
    half = pl.pallas_call(
        functools.partial(kernel, n, local, surfaces),
        out_shape=jax.ShapeDtypeStruct(state.shape, jnp.float32),
        in_specs=[pl.BlockSpec(memory_space=pltpu.HBM)] * 3,
        out_specs=pl.BlockSpec(memory_space=pltpu.VMEM),
        scratch_shapes=[
            pltpu.VMEM(state.shape, jnp.float32),
            pltpu.SMEM(donor_rows.shape, jnp.int32),
            pltpu.SMEM(donor_weights.shape, jnp.float32),
            pltpu.VMEM((2, 4, rows + 4, 8, columns), jnp.float32),
            pltpu.VMEM((2, 4, rows, 8, columns), jnp.float32),
            pltpu.VMEM((n, 8, LANES), jnp.float32),
            pltpu.VMEM((n, 8, LANES), jnp.float32),
            pltpu.VMEM((4, rows + 4, 8, columns), jnp.float32),
            pltpu.VMEM((4, rows, 8, columns), jnp.float32),
            pltpu.VMEM((2, 4, 8, LANES), jnp.float32),
            pltpu.SemaphoreType.DMA((3,)),
            pltpu.SemaphoreType.DMA((2, 4)),
            pltpu.SemaphoreType.DMA((2, 4)),
        ],
        compiler_params=pltpu.CompilerParams(
            collective_id=0, has_side_effects=True, vmem_limit_bytes=24 * 2**20
        ),
    )(*inputs)
    return state - (2.0 * time_step) * half, half + half


def solution(mesh):
    return jax.shard_map(
        functools.partial(per_device, mesh.shape["mesh"]),
        mesh=mesh,
        in_specs=(
            P(("parts", "inst"), None, None, "mesh", None),
            P("inst", None, None, "mesh"),
            P("inst", None, None, "mesh"),
        ),
        out_specs=(
            P(("parts", "inst"), None, None, "mesh", None),
            P(("parts", "inst"), None, None, "mesh", None),
        ),
        check_vma=False,
    )
```

```python
import functools
import math

import jax
import jax.numpy as jnp
from jax import lax
from jax.experimental import pallas as pl
from jax.experimental.pallas import tpu as pltpu
from jax.sharding import PartitionSpec as P

heat_ratio = 1.4
second_coef = 0.5
fourth_coef = 1.0 / 32.0
time_step = 0.05
LANES = 128
MESH = pl.DeviceIdType.MESH


def spectral(offset, total):
    if offset % total == 0:
        return 0.0
    angle = math.pi * offset / total
    return 0.5 * (1.0 - 2.0 * (offset % 2)) * math.cos(angle) / math.sin(angle)


def primitives(value):
    density, axial, circ, energy = value
    inverse = 1.0 / density
    speed_one = axial * inverse
    speed_two = circ * inverse
    pressure = (heat_ratio - 1.0) * (energy - 0.5 * (axial * speed_one + circ * speed_two))
    sound = jnp.sqrt(heat_ratio * pressure * inverse)
    return pressure, sound, speed_one, speed_two


def flux(value, pressure, speed, normal):
    density, axial, circ, energy = value
    return [
        axial if normal == 1 else circ,
        axial * speed + pressure if normal == 1 else axial * speed,
        circ * speed + pressure if normal == 2 else circ * speed,
        (energy + pressure) * speed,
    ]


def sensor(before, center, after):
    twice = 2.0 * center
    return jnp.abs(after - twice + before) / (after + twice + before)


def face(cells, sensors, radii, fluxes):
    eps_two = second_coef * jnp.maximum(sensors[0], sensors[1])
    eps_four = jnp.maximum(0.0, fourth_coef - eps_two)
    radius = 0.5 * (radii[0] + radii[1])
    two = radius * eps_two
    four = radius * eps_four
    out = []
    for c in range(4):
        step = cells[2][c] - cells[1][c]
        third_diff = cells[3][c] - cells[0][c] - 3.0 * step
        out.append(0.5 * (fluxes[0][c] + fluxes[1][c]) - two * step + four * third_diff)
    return out


def lane_roll(value, shift):
    shift = shift % LANES
    return value if shift == 0 else pltpu.roll(value, shift, 1)


def kernel(
    n, local, surfaces, state_in, rows_in, weights_in, half_ref,
    state_ref, rows_ref, weights_ref, field, other, packed_one, packed_two, prims, acc, edges,
    local_sem, send_sem, recv_sem,
):
    me = lax.axis_index("mesh")
    inst = lax.axis_index("inst")
    partner = 1 - inst
    rows = state_ref.shape[3]
    packed = (packed_one, packed_two)
    lane = lax.broadcasted_iota(jnp.int32, (8, LANES), 1)
    sub = lax.broadcasted_iota(jnp.int32, (8, LANES), 0)
    wide_sub = lax.broadcasted_iota(jnp.int32, (8, 2 * LANES), 0)

    loads = [
        pltpu.make_async_copy(source, target, local_sem.at[i])
        for i, (source, target) in enumerate(
            ((state_in, state_ref), (rows_in, rows_ref), (weights_in, weights_ref))
        )
    ]
    for load in loads:
        load.start()
    barrier = pltpu.get_barrier_semaphore()

    def greet(k, carry):
        pl.semaphore_signal(
            barrier, inc=1, device_id={"mesh": lax.rem(me + k, n)}, device_id_type=MESH
        )
        return carry

    pl.semaphore_signal(barrier, inc=1, device_id={"inst": partner}, device_id_type=MESH)
    lax.fori_loop(1, n, greet, 0)

    loads[0].wait()
    for c in range(4):
        block = jnp.stack([state_ref[t, c, s] for t in range(local) for s in range(surfaces)])
        field[0, c, 2 : 2 + rows] = jnp.swapaxes(block, 0, 1)

    place = lane % 4
    lane_row = lane // 16

    def donor_weights():
        loads[1].wait()
        loads[2].wait()
        weight = []
        for point in range(2):
            total = jnp.zeros((8, LANES), jnp.float32)
            for t in range(local):
                for side in range(2):
                    mine = jnp.zeros((8, LANES), jnp.float32)
                    for r in range(rows):
                        mine = jnp.where(lane_row == r, weights_ref[t, side, point, r], mine)
                    inside = (sub // surfaces == t) & ((place >= 2) if side == 0 else (place < 2))
                    total = jnp.where(inside, mine, total)
            weight.append(total)
        return weight

    def coefficients(offsets):
        out = jnp.zeros((8, 2 * LANES), jnp.float32)
        for t in range(local):
            out = jnp.where(wide_sub // surfaces == t, spectral(offsets[t], 2 * local), out)
        return out

    own_coef = [None] + [
        coefficients([t - (t - k) % local for t in range(local)]) for k in range(1, local)
    ]
    other_coef = [
        coefficients([local + t - (t - k) % local for t in range(local)]) for k in range(local)
    ]

    spot = lane % 16

    def pack_rows(section, out, which):
        for r in which:
            for c in range(4):
                rotor = field[section, c, 2 + r, :, 0:LANES]
                stator = field[section, c, 2 + r, :, LANES : 2 * LANES]
                edge = lane_roll(jnp.where(lane < 64, stator, rotor), r * 16 + 3)
                out[c] = edge if out[c] is None else jnp.where(lane_row == r, edge, out[c])
        return out

    def pack_end(section, out):
        for c in range(4):
            edges[section, c] = out[c]
        total = lane_roll(out[0], -1)
        for c in range(1, 4):
            total = jnp.where(spot // 4 == c, lane_roll(out[c], c * 4 - 1), total)
        packed[section][me] = total

    def copies(section):
        down = lax.rem(me + n - 1, n)
        up = lax.rem(me + 1, n)
        top = pltpu.make_async_remote_copy(
            field.at[section, :, rows : rows + 2], field.at[section, :, 0:2],
            send_sem.at[section, 0], recv_sem.at[section, 0],
            device_id={"mesh": up}, device_id_type=MESH,
        )
        bottom = pltpu.make_async_remote_copy(
            field.at[section, :, 2:4], field.at[section, :, rows + 2 : rows + 4],
            send_sem.at[section, 1], recv_sem.at[section, 1],
            device_id={"mesh": down}, device_id_type=MESH,
        )
        cross = pltpu.make_async_remote_copy(
            field.at[section, :, 2 : 2 + rows], other.at[section],
            send_sem.at[section, 2], recv_sem.at[section, 2],
            device_id={"inst": partner}, device_id_type=MESH,
        )
        return top, bottom, cross

    def send_columns(section):
        def one(k, carry):
            pltpu.make_async_remote_copy(
                packed[section].at[me], packed[section].at[me],
                send_sem.at[section, 3], recv_sem.at[section, 3],
                device_id={"mesh": lax.rem(me + k, n)}, device_id_type=MESH,
            ).start()
            return carry

        lax.fori_loop(1, n, one, 0)

    def all_columns(section):
        return pltpu.make_async_remote_copy(
            packed[section].at[0 : n - 1], packed[section].at[0 : n - 1],
            send_sem.at[section, 3], recv_sem.at[section, 3],
            device_id={"inst": partner}, device_id_type=MESH,
        )

    def interpolate(section, weight):
        donors = [jnp.zeros((8, LANES), jnp.float32)] * 2
        for t in range(local):
            for side in range(2):
                start = rows_ref[t, side, 0, 0]
                block = start // rows
                offset = start - block * rows
                low = packed[section][block]
                high = packed[section][lax.rem(block + 1, n)]
                inside = (sub // surfaces == t) & ((place >= 2) if side == 0 else (place < 2))
                for point in range(2):
                    shift = (offset + point) * 16
                    picked = jnp.where(lane >= shift, low, high)
                    picked = pltpu.roll(picked, lax.rem(LANES - shift, LANES), 1)
                    donors[point] = jnp.where(inside, picked, donors[point])
        total = weight[0] * donors[0] + weight[1] * donors[1]
        window = []
        for c in range(4):
            near = edges[section, c]
            value = jnp.where(spot < 3, near, lane_roll(near, 7))
            value = jnp.where((spot == 3) | (spot == 4), lane_roll(total, 1 - 4 * c), value)
            value = jnp.where((spot == 8) | (spot == 9), lane_roll(total, 8 - 4 * c), value)
            window.append(jnp.where((spot < 5) | ((spot >= 8) & (spot < 13)), value, near_one[c]))
        pressure, sound, speed, _ = primitives(window)
        radius = jnp.abs(speed) + sound
        flow = flux(window, pressure, speed, 1)
        sense = sensor(lane_roll(pressure, 1), pressure, lane_roll(pressure, -1))
        edge_face = face(
            [moved(window, 1), window, moved(window, -1), moved(window, -2)],
            [sense, lane_roll(sense, -1)],
            [radius, lane_roll(radius, -1)],
            [flow, moved(flow, -1)],
        )
        valid = (spot == 1) | (spot == 2) | (spot == 9) | (spot == 10)
        fix = []
        for c in range(4):
            value = jnp.where(valid, edge_face[c], 0.0)
            value = value - lane_roll(value, 1)
            fix.append(jnp.where(spot < 3, value, lane_roll(value, -7)))
        for c in range(4):
            for r in range(rows):
                moved_back = lane_roll(fix[c], -(r * 16 + 3))
                acc[c, r, :, 0:LANES] += jnp.where(lane >= LANES - 2, moved_back, 0.0)
                acc[c, r, :, LANES : 2 * LANES] += jnp.where(lane < 2, moved_back, 0.0)

    near_one = [1.0, 0.0, 0.0, 2.0]

    def moved(value, shift):
        return [lane_roll(v, shift) for v in value]

    def store_primitives(section, row):
        value = [field[section, c, row] for c in range(4)]
        for i, item in enumerate(primitives(value)):
            prims[i, row] = item

    def row_sensor(row):
        return sensor(prims[0, row - 1], prims[0, row], prims[0, row + 1])

    def circ_face(section, row, before):
        after = row_sensor(row + 1)
        cells = [[field[section, c, row + k] for c in range(4)] for k in (-1, 0, 1, 2)]
        speeds = [prims[3, row + k] for k in (0, 1)]
        radii = [jnp.abs(speeds[k]) + prims[1, row + k] for k in (0, 1)]
        fluxes = [flux(cells[1 + k], prims[0, row + k], speeds[k], 2) for k in (0, 1)]
        return face(cells, [before, after], radii, fluxes), after

    def axial_half(section, row, h):
        cut = slice(h * LANES, (h + 1) * LANES)
        value = [field[section, c, row + 2, :, cut] for c in range(4)]
        pressure = prims[0, row + 2, :, cut]
        speed = prims[2, row + 2, :, cut]
        radius = jnp.abs(speed) + prims[1, row + 2, :, cut]
        flow = flux(value, pressure, speed, 1)
        first, last = lane == 0, lane == LANES - 1

        def before(own):
            return jnp.where(first, own, lane_roll(own, 1)) if h == 0 else lane_roll(own, 1)

        def after(own):
            return jnp.where(last, own, lane_roll(own, -1)) if h == 1 else lane_roll(own, -1)

        following = [after(v) for v in value]
        second = moved(value, -2)
        if h == 1:
            second = [jnp.where(lane >= LANES - 2, a, b) for a, b in zip(following, second)]
        sense = sensor(before(pressure), pressure, after(pressure))
        sense_after = lane_roll(sense, -1)
        if h == 1:
            sense_after = jnp.where(last, 0.0, sense_after)
        right = face(
            [[before(v) for v in value], value, following, second],
            [sense, sense_after],
            [radius, after(radius)],
            [flow, [after(f) for f in flow]],
        )
        keep = lane < LANES - 2 if h == 0 else lane > 0
        right = [jnp.where(keep, f, 0.0) for f in right]
        if h == 0:
            four = radius * jnp.maximum(0.0, fourth_coef - second_coef * sense)
            start = [flow[c] + four * (following[c] - value[c]) for c in range(4)]
        else:
            start = [0.0] * 4
        return [right[c] - jnp.where(first, start[c], lane_roll(right[c], 1)) for c in range(4)]

    def source(values, coefs, total):
        for k, coef in enumerate(coefs):
            if coef is not None:
                value = values if k == 0 else pltpu.roll(values, surfaces * k, 0)
                total = coef * value if total is None else total + coef * value
        return total

    def alone(section):
        def one(row, carry):
            store_primitives(section, row + 2)
            halves = [axial_half(section, row, h) for h in range(2)]
            for c in range(4):
                term = jnp.concatenate([halves[0][c], halves[1][c]], axis=1)
                acc[c, row] = source(field[section, c, row + 2], own_coef, term)
            return carry

        lax.fori_loop(0, rows, one, 0, unroll=2)

        def inner(row, carry):
            left, sense = carry
            right, sense = circ_face(section, row + 2, sense)
            for c in range(4):
                acc[c, row] += right[c] - left[c]
            return right, sense

        zero = [jnp.zeros((8, 2 * LANES), jnp.float32)] * 4
        left, _ = lax.fori_loop(1, rows - 2, inner, (zero, row_sensor(3)))
        for c in range(4):
            acc[c, rows - 2] -= left[c]

    def finish(section, row, extra=None):
        for c in range(4):
            total = acc[c, row] if extra is None else acc[c, row] + extra[c]
            if section == 0:
                field[1, c, row + 2] = field[0, c, row + 2] - 0.5 * time_step * total
            else:
                acc[c, row] = 0.5 * total

    def together(section, weight):
        top, bottom, cross = copies(section)
        cross.wait_recv()

        def others(row, carry):
            for c in range(4):
                acc[c, row] = source(other[section, c, row], other_coef, acc[c, row])
            return carry

        lax.fori_loop(0, rows, others, 0, unroll=2)
        all_columns(section).wait_recv()
        interpolate(section, weight)
        for row in range(2, rows - 2):
            finish(section, row)
        out = [None] * 4
        if section == 0:
            next_top, next_bottom, next_cross = copies(1)
            out = pack_rows(1, out, range(2, rows - 2))
        top.wait_recv()
        for row in (0, 1):
            store_primitives(section, row)
        first, sense = circ_face(section, 1, row_sensor(1))
        second, _ = circ_face(section, 2, sense)
        finish(section, 0, [second[c] - first[c] for c in range(4)])
        finish(section, 1, [-second[c] for c in range(4)])
        if section == 0:
            out = pack_rows(1, out, (0, 1))
        bottom.wait_recv()
        for row in (rows + 2, rows + 3):
            store_primitives(section, row)
        first, sense = circ_face(section, rows, row_sensor(rows))
        second, _ = circ_face(section, rows + 1, sense)
        finish(section, rows - 2, first)
        finish(section, rows - 1, [second[c] - first[c] for c in range(4)])
        if section == 0:
            pack_end(1, pack_rows(1, out, (rows - 2, rows - 1)))
            send_columns(1)
            next_bottom.start()
            next_top.start()
            next_cross.start()

    pack_end(0, pack_rows(0, [None] * 4, range(rows)))
    pl.semaphore_wait(barrier, n)
    send_columns(0)
    for copy in copies(0):
        copy.start()
    weight = donor_weights()
    alone(0)
    together(0, weight)
    alone(1)
    together(1, weight)
    for c in range(4):
        block = jnp.swapaxes(acc[c], 0, 1)
        for t in range(local):
            for s in range(surfaces):
                half_ref[t, c, s] = block[t * surfaces + s]
    for section in range(2):
        for copy in copies(section):
            copy.wait_send()
        all_columns(section).wait_send()


def per_device(n, state, donor_rows, donor_weights):
    local, _, surfaces, rows, columns = state.shape
    inputs = [
        pltpu.with_memory_space_constraint(x, pltpu.HBM)
        for x in (state, donor_rows, donor_weights)
    ]
    half = pl.pallas_call(
        functools.partial(kernel, n, local, surfaces),
        out_shape=jax.ShapeDtypeStruct(state.shape, jnp.float32),
        in_specs=[pl.BlockSpec(memory_space=pltpu.HBM)] * 3,
        out_specs=pl.BlockSpec(memory_space=pltpu.VMEM),
        scratch_shapes=[
            pltpu.VMEM(state.shape, jnp.float32),
            pltpu.SMEM(donor_rows.shape, jnp.int32),
            pltpu.SMEM(donor_weights.shape, jnp.float32),
            pltpu.VMEM((2, 4, rows + 4, 8, columns), jnp.float32),
            pltpu.VMEM((2, 4, rows, 8, columns), jnp.float32),
            pltpu.VMEM((n, 8, LANES), jnp.float32),
            pltpu.VMEM((n, 8, LANES), jnp.float32),
            pltpu.VMEM((4, rows + 4, 8, columns), jnp.float32),
            pltpu.VMEM((4, rows, 8, columns), jnp.float32),
            pltpu.VMEM((2, 4, 8, LANES), jnp.float32),
            pltpu.SemaphoreType.DMA((3,)),
            pltpu.SemaphoreType.DMA((2, 4)),
            pltpu.SemaphoreType.DMA((2, 4)),
        ],
        compiler_params=pltpu.CompilerParams(
            collective_id=0, has_side_effects=True, vmem_limit_bytes=24 * 2**20
        ),
    )(*inputs)
    return state - (2.0 * time_step) * half, half + half


def solution(mesh):
    return jax.shard_map(
        functools.partial(per_device, mesh.shape["mesh"]),
        mesh=mesh,
        in_specs=(
            P(("parts", "inst"), None, None, "mesh", None),
            P("inst", None, None, "mesh"),
            P("inst", None, None, "mesh"),
        ),
        out_specs=(
            P(("parts", "inst"), None, None, "mesh", None),
            P(("parts", "inst"), None, None, "mesh", None),
        ),
        check_vma=False,
    )
```

```python
import functools
import math

import jax
import jax.numpy as jnp
from jax import lax
from jax.experimental import pallas as pl
from jax.experimental.pallas import tpu as pltpu
from jax.sharding import PartitionSpec as P

heat_ratio = 1.4
second_coef = 0.5
fourth_coef = 1.0 / 32.0
time_step = 0.05
LANES = 128
MESH = pl.DeviceIdType.MESH


def spectral(offset, total):
    if offset % total == 0:
        return 0.0
    angle = math.pi * offset / total
    return 0.5 * (1.0 - 2.0 * (offset % 2)) * math.cos(angle) / math.sin(angle)


def primitives(value):
    density, axial, circ, energy = value
    inverse = 1.0 / density
    speed_one = axial * inverse
    speed_two = circ * inverse
    pressure = (heat_ratio - 1.0) * (energy - 0.5 * (axial * speed_one + circ * speed_two))
    sound = jnp.sqrt(heat_ratio * pressure * inverse)
    return pressure, sound, speed_one, speed_two


def flux(value, pressure, speed, normal):
    density, axial, circ, energy = value
    return [
        axial if normal == 1 else circ,
        axial * speed + pressure if normal == 1 else axial * speed,
        circ * speed + pressure if normal == 2 else circ * speed,
        (energy + pressure) * speed,
    ]


def sensor(before, center, after):
    twice = 2.0 * center
    return jnp.abs(after - twice + before) / (after + twice + before)


def face(cells, sensors, radii, fluxes):
    eps_two = second_coef * jnp.maximum(sensors[0], sensors[1])
    eps_four = jnp.maximum(0.0, fourth_coef - eps_two)
    radius = 0.5 * (radii[0] + radii[1])
    two = radius * eps_two
    four = radius * eps_four
    out = []
    for c in range(4):
        step = cells[2][c] - cells[1][c]
        third_diff = cells[3][c] - cells[0][c] - 3.0 * step
        out.append(0.5 * (fluxes[0][c] + fluxes[1][c]) - two * step + four * third_diff)
    return out


def lane_roll(value, shift):
    shift = shift % LANES
    return value if shift == 0 else pltpu.roll(value, shift, 1)


def kernel(
    n, local, surfaces, state_in, rows_in, weights_in, half_ref,
    state_ref, rows_ref, weights_ref, field, other, packed_one, packed_two, prims, acc, edges,
    local_sem, send_sem, recv_sem,
):
    me = lax.axis_index("mesh")
    inst = lax.axis_index("inst")
    partner = 1 - inst
    rows = state_ref.shape[3]
    packed = (packed_one, packed_two)
    lane = lax.broadcasted_iota(jnp.int32, (8, LANES), 1)
    sub = lax.broadcasted_iota(jnp.int32, (8, LANES), 0)
    wide_sub = lax.broadcasted_iota(jnp.int32, (8, 2 * LANES), 0)

    loads = [
        pltpu.make_async_copy(source, target, local_sem.at[i])
        for i, (source, target) in enumerate(
            ((state_in, state_ref), (rows_in, rows_ref), (weights_in, weights_ref))
        )
    ]
    for load in loads:
        load.start()
    barrier = pltpu.get_barrier_semaphore()

    def greet(k, carry):
        pl.semaphore_signal(
            barrier, inc=1, device_id={"mesh": lax.rem(me + k, n)}, device_id_type=MESH
        )
        return carry

    pl.semaphore_signal(barrier, inc=1, device_id={"inst": partner}, device_id_type=MESH)
    lax.fori_loop(1, n, greet, 0)

    loads[0].wait()
    for c in range(4):
        block = jnp.stack([state_ref[t, c, s] for t in range(local) for s in range(surfaces)])
        field[0, c, 2 : 2 + rows] = jnp.swapaxes(block, 0, 1)

    place = lane % 4
    lane_row = lane // 16

    def donor_weights():
        loads[1].wait()
        loads[2].wait()
        weight = []
        for point in range(2):
            total = jnp.zeros((8, LANES), jnp.float32)
            for t in range(local):
                for side in range(2):
                    mine = jnp.zeros((8, LANES), jnp.float32)
                    for r in range(rows):
                        mine = jnp.where(lane_row == r, weights_ref[t, side, point, r], mine)
                    inside = (sub // surfaces == t) & ((place >= 2) if side == 0 else (place < 2))
                    total = jnp.where(inside, mine, total)
            weight.append(total)
        return weight

    def coefficients(offsets):
        out = jnp.zeros((8, 2 * LANES), jnp.float32)
        for t in range(local):
            out = jnp.where(wide_sub // surfaces == t, spectral(offsets[t], 2 * local), out)
        return out

    own_coef = [None] + [
        coefficients([t - (t - k) % local for t in range(local)]) for k in range(1, local)
    ]
    other_coef = [
        coefficients([local + t - (t - k) % local for t in range(local)]) for k in range(local)
    ]

    spot = lane % 16

    def pack_rows(section, out, which):
        for r in which:
            for c in range(4):
                rotor = field[section, c, 2 + r, :, 0:LANES]
                stator = field[section, c, 2 + r, :, LANES : 2 * LANES]
                edge = lane_roll(jnp.where(lane < 64, stator, rotor), r * 16 + 3)
                out[c] = edge if out[c] is None else jnp.where(lane_row == r, edge, out[c])
        return out

    def pack_end(section, out):
        for c in range(4):
            edges[section, c] = out[c]
        total = lane_roll(out[0], -1)
        for c in range(1, 4):
            total = jnp.where(spot // 4 == c, lane_roll(out[c], c * 4 - 1), total)
        packed[section][me] = total

    def copies(section):
        down = lax.rem(me + n - 1, n)
        up = lax.rem(me + 1, n)
        top = pltpu.make_async_remote_copy(
            field.at[section, :, rows : rows + 2], field.at[section, :, 0:2],
            send_sem.at[section, 0], recv_sem.at[section, 0],
            device_id={"mesh": up}, device_id_type=MESH,
        )
        bottom = pltpu.make_async_remote_copy(
            field.at[section, :, 2:4], field.at[section, :, rows + 2 : rows + 4],
            send_sem.at[section, 1], recv_sem.at[section, 1],
            device_id={"mesh": down}, device_id_type=MESH,
        )
        cross = pltpu.make_async_remote_copy(
            field.at[section, :, 2 : 2 + rows], other.at[section],
            send_sem.at[section, 2], recv_sem.at[section, 2],
            device_id={"inst": partner}, device_id_type=MESH,
        )
        return top, bottom, cross

    def send_columns(section):
        def one(k, carry):
            low = jnp.where(me < n // 2, 1, 0)
            rank = low * (n - 1 - me) + (1 - low) * me
            spot_k = k + jnp.where(k >= rank, 1, 0)
            target = low * (n - 1 - spot_k) + (1 - low) * spot_k
            pltpu.make_async_remote_copy(
                packed[section].at[me], packed[section].at[me],
                send_sem.at[section, 3], recv_sem.at[section, 3],
                device_id={"mesh": target}, device_id_type=MESH,
            ).start()
            return carry

        lax.fori_loop(0, n - 1, one, 0)

    def all_columns(section):
        return pltpu.make_async_remote_copy(
            packed[section].at[0 : n - 1], packed[section].at[0 : n - 1],
            send_sem.at[section, 3], recv_sem.at[section, 3],
            device_id={"inst": partner}, device_id_type=MESH,
        )

    def interpolate(section, weight):
        donors = [jnp.zeros((8, LANES), jnp.float32)] * 2
        for t in range(local):
            for side in range(2):
                start = rows_ref[t, side, 0, 0]
                block = start // rows
                offset = start - block * rows
                low = packed[section][block]
                high = packed[section][lax.rem(block + 1, n)]
                inside = (sub // surfaces == t) & ((place >= 2) if side == 0 else (place < 2))
                for point in range(2):
                    shift = (offset + point) * 16
                    picked = jnp.where(lane >= shift, low, high)
                    picked = pltpu.roll(picked, lax.rem(LANES - shift, LANES), 1)
                    donors[point] = jnp.where(inside, picked, donors[point])
        total = weight[0] * donors[0] + weight[1] * donors[1]
        window = []
        for c in range(4):
            near = edges[section, c]
            value = jnp.where(spot < 3, near, lane_roll(near, 7))
            value = jnp.where((spot == 3) | (spot == 4), lane_roll(total, 1 - 4 * c), value)
            value = jnp.where((spot == 8) | (spot == 9), lane_roll(total, 8 - 4 * c), value)
            window.append(jnp.where((spot < 5) | ((spot >= 8) & (spot < 13)), value, near_one[c]))
        pressure, sound, speed, _ = primitives(window)
        radius = jnp.abs(speed) + sound
        flow = flux(window, pressure, speed, 1)
        sense = sensor(lane_roll(pressure, 1), pressure, lane_roll(pressure, -1))
        edge_face = face(
            [moved(window, 1), window, moved(window, -1), moved(window, -2)],
            [sense, lane_roll(sense, -1)],
            [radius, lane_roll(radius, -1)],
            [flow, moved(flow, -1)],
        )
        valid = (spot == 1) | (spot == 2) | (spot == 9) | (spot == 10)
        fix = []
        for c in range(4):
            value = jnp.where(valid, edge_face[c], 0.0)
            value = value - lane_roll(value, 1)
            fix.append(jnp.where(spot < 3, value, lane_roll(value, -7)))
        for c in range(4):
            for r in range(rows):
                moved_back = lane_roll(fix[c], -(r * 16 + 3))
                acc[c, r, :, 0:LANES] += jnp.where(lane >= LANES - 2, moved_back, 0.0)
                acc[c, r, :, LANES : 2 * LANES] += jnp.where(lane < 2, moved_back, 0.0)

    near_one = [1.0, 0.0, 0.0, 2.0]

    def moved(value, shift):
        return [lane_roll(v, shift) for v in value]

    def store_primitives(section, row):
        value = [field[section, c, row] for c in range(4)]
        for i, item in enumerate(primitives(value)):
            prims[i, row] = item

    def row_sensor(row):
        return sensor(prims[0, row - 1], prims[0, row], prims[0, row + 1])

    def circ_face(section, row, before):
        after = row_sensor(row + 1)
        cells = [[field[section, c, row + k] for c in range(4)] for k in (-1, 0, 1, 2)]
        speeds = [prims[3, row + k] for k in (0, 1)]
        radii = [jnp.abs(speeds[k]) + prims[1, row + k] for k in (0, 1)]
        fluxes = [flux(cells[1 + k], prims[0, row + k], speeds[k], 2) for k in (0, 1)]
        return face(cells, [before, after], radii, fluxes), after

    def axial_half(section, row, h):
        cut = slice(h * LANES, (h + 1) * LANES)
        value = [field[section, c, row + 2, :, cut] for c in range(4)]
        pressure = prims[0, row + 2, :, cut]
        speed = prims[2, row + 2, :, cut]
        radius = jnp.abs(speed) + prims[1, row + 2, :, cut]
        flow = flux(value, pressure, speed, 1)
        first, last = lane == 0, lane == LANES - 1

        def before(own):
            return jnp.where(first, own, lane_roll(own, 1)) if h == 0 else lane_roll(own, 1)

        def after(own):
            return jnp.where(last, own, lane_roll(own, -1)) if h == 1 else lane_roll(own, -1)

        following = [after(v) for v in value]
        second = moved(value, -2)
        if h == 1:
            second = [jnp.where(lane >= LANES - 2, a, b) for a, b in zip(following, second)]
        sense = sensor(before(pressure), pressure, after(pressure))
        sense_after = lane_roll(sense, -1)
        if h == 1:
            sense_after = jnp.where(last, 0.0, sense_after)
        right = face(
            [[before(v) for v in value], value, following, second],
            [sense, sense_after],
            [radius, after(radius)],
            [flow, [after(f) for f in flow]],
        )
        keep = lane < LANES - 2 if h == 0 else lane > 0
        right = [jnp.where(keep, f, 0.0) for f in right]
        if h == 0:
            four = radius * jnp.maximum(0.0, fourth_coef - second_coef * sense)
            start = [flow[c] + four * (following[c] - value[c]) for c in range(4)]
        else:
            start = [0.0] * 4
        return [right[c] - jnp.where(first, start[c], lane_roll(right[c], 1)) for c in range(4)]

    def source(values, coefs, total):
        for k, coef in enumerate(coefs):
            if coef is not None:
                value = values if k == 0 else pltpu.roll(values, surfaces * k, 0)
                total = coef * value if total is None else total + coef * value
        return total

    def start_halos(section):
        top, bottom, cross = copies(section)

        @pl.when(me < n // 2)
        def _():
            bottom.start()
            top.start()

        @pl.when(me >= n // 2)
        def _():
            top.start()
            bottom.start()

        cross.start()

    def alone(section):
        def one(row, carry):
            store_primitives(section, row + 2)
            halves = [axial_half(section, row, h) for h in range(2)]
            for c in range(4):
                term = jnp.concatenate([halves[0][c], halves[1][c]], axis=1)
                acc[c, row] = source(field[section, c, row + 2], own_coef, term)
            return carry

        lax.fori_loop(0, rows, one, 0, unroll=2)

        def inner(row, carry):
            left, sense = carry
            right, sense = circ_face(section, row + 2, sense)
            for c in range(4):
                acc[c, row] += right[c] - left[c]
            return right, sense

        zero = [jnp.zeros((8, 2 * LANES), jnp.float32)] * 4
        left, _ = lax.fori_loop(1, rows - 2, inner, (zero, row_sensor(3)))
        for c in range(4):
            acc[c, rows - 2] -= left[c]

    def finish(section, row, extra=None):
        for c in range(4):
            total = acc[c, row] if extra is None else acc[c, row] + extra[c]
            if section == 0:
                field[1, c, row + 2] = field[0, c, row + 2] - 0.5 * time_step * total
            else:
                acc[c, row] = 0.5 * total

    def together(section, weight):
        top, bottom, cross = copies(section)
        cross.wait_recv()

        def others(row, carry):
            for c in range(4):
                acc[c, row] = source(other[section, c, row], other_coef, acc[c, row])
            return carry

        lax.fori_loop(0, rows, others, 0, unroll=2)
        all_columns(section).wait_recv()
        interpolate(section, weight)
        for row in range(2, rows - 2):
            finish(section, row)
        out = [None] * 4
        if section == 0:
            out = pack_rows(1, out, range(2, rows - 2))
        top.wait_recv()
        for row in (0, 1):
            store_primitives(section, row)
        first, sense = circ_face(section, 1, row_sensor(1))
        second, _ = circ_face(section, 2, sense)
        finish(section, 0, [second[c] - first[c] for c in range(4)])
        finish(section, 1, [-second[c] for c in range(4)])
        if section == 0:
            out = pack_rows(1, out, (0, 1))
        bottom.wait_recv()
        for row in (rows + 2, rows + 3):
            store_primitives(section, row)
        first, sense = circ_face(section, rows, row_sensor(rows))
        second, _ = circ_face(section, rows + 1, sense)
        finish(section, rows - 2, first)
        finish(section, rows - 1, [second[c] - first[c] for c in range(4)])
        if section == 0:
            pack_end(1, pack_rows(1, out, (rows - 2, rows - 1)))
            send_columns(1)
            start_halos(1)

    pack_end(0, pack_rows(0, [None] * 4, range(rows)))
    pl.semaphore_wait(barrier, n)
    send_columns(0)
    start_halos(0)
    weight = donor_weights()
    alone(0)
    together(0, weight)
    alone(1)
    together(1, weight)
    for c in range(4):
        block = jnp.swapaxes(acc[c], 0, 1)
        for t in range(local):
            for s in range(surfaces):
                half_ref[t, c, s] = block[t * surfaces + s]
    for section in range(2):
        for copy in copies(section):
            copy.wait_send()
        all_columns(section).wait_send()


def per_device(n, state, donor_rows, donor_weights):
    local, _, surfaces, rows, columns = state.shape
    inputs = [
        pltpu.with_memory_space_constraint(x, pltpu.HBM)
        for x in (state, donor_rows, donor_weights)
    ]
    half = pl.pallas_call(
        functools.partial(kernel, n, local, surfaces),
        out_shape=jax.ShapeDtypeStruct(state.shape, jnp.float32),
        in_specs=[pl.BlockSpec(memory_space=pltpu.HBM)] * 3,
        out_specs=pl.BlockSpec(memory_space=pltpu.VMEM),
        scratch_shapes=[
            pltpu.VMEM(state.shape, jnp.float32),
            pltpu.SMEM(donor_rows.shape, jnp.int32),
            pltpu.SMEM(donor_weights.shape, jnp.float32),
            pltpu.VMEM((2, 4, rows + 4, 8, columns), jnp.float32),
            pltpu.VMEM((2, 4, rows, 8, columns), jnp.float32),
            pltpu.VMEM((n, 8, LANES), jnp.float32),
            pltpu.VMEM((n, 8, LANES), jnp.float32),
            pltpu.VMEM((4, rows + 4, 8, columns), jnp.float32),
            pltpu.VMEM((4, rows, 8, columns), jnp.float32),
            pltpu.VMEM((2, 4, 8, LANES), jnp.float32),
            pltpu.SemaphoreType.DMA((3,)),
            pltpu.SemaphoreType.DMA((2, 4)),
            pltpu.SemaphoreType.DMA((2, 4)),
        ],
        compiler_params=pltpu.CompilerParams(
            collective_id=0, has_side_effects=True, vmem_limit_bytes=24 * 2**20
        ),
    )(*inputs)
    return state - (2.0 * time_step) * half, half + half


def solution(mesh):
    return jax.shard_map(
        functools.partial(per_device, mesh.shape["mesh"]),
        mesh=mesh,
        in_specs=(
            P(("parts", "inst"), None, None, "mesh", None),
            P("inst", None, None, "mesh"),
            P("inst", None, None, "mesh"),
        ),
        out_specs=(
            P(("parts", "inst"), None, None, "mesh", None),
            P(("parts", "inst"), None, None, "mesh", None),
        ),
        check_vma=False,
    )
```
